512 devices in a mesh: sp: 32 (over x, z_lo, core), ch: 16 (over y, z_hi).
Axes of the slice: x: 4, y: 8, z: 8 (z_hi: 2, z_lo: 4; z = z_hi * 4 + z_lo), core: 2. Of those that a mesh axis runs over, the one named last changes fastest.
Arguments:
- volume: bfloat16 [256, 64, 8, 128], P('ch', 'sp'), may hold values from -6 to 6
- filters: bfloat16 [256, 3, 3, 3, 256], P('ch'), may hold values from -0.078125 to 0.078125
- cotangent: bfloat16 [256, 64, 8, 128], P('ch', 'sp'), may hold values from -6 to 6
Outputs:
- response: bfloat16 [256, 64, 8, 128], P('ch', 'sp')
- input_grad: bfloat16 [256, 64, 8, 128], P('ch', 'sp')
- filter_grad: bfloat16 [256, 3, 3, 3, 256], P('ch')
The draws below stay inside these ranges and needn't reach their ends.
All inputs are finite; a program needn't handle non-finite values.
Results may differ from the reference program's by a relative error of at most 0.0024.
Values may be sent and summed in bfloat16 or wider, within the bound.
No kernel may reach another device: no remote copies, remote signals or barrier semaphores. Data moves between devices by JAX's collectives and lax.ppermute only.
A program may use at most 64 MiB of HBM per device.

```python
import math
import jax
import jax.numpy as jnp
from jax import lax

C = 256
F = 256
HEIGHT = 8
WIDTH = 128
DEPTH = 64


def shard_levels(stream_key, shape, cuts, least, high):
    level, own = 1.0, jax.random.fold_in(stream_key, 6)
    for dim, blocks in cuts:
        heights = jnp.exp(jax.random.uniform(jax.random.fold_in(own, dim), (blocks,), jnp.float32, least / len(cuts), high / len(cuts)))
        level = level * jnp.repeat(heights, shape[dim] // blocks).reshape([-1 if axis == dim else 1 for axis in range(len(shape))])
    return level


def scatter_about(rng, shape, width, most, split=(), kind=jnp.bfloat16):
    entries = jax.random.normal(rng, shape, jnp.float32) * width
    if len(split) > 0:
        entries = shard_levels(rng, shape, split, -0.22, 0.18) * entries
    return jnp.clip(entries, min=-most, max=most).astype(kind)


def setup_inputs(seed: int = 0) -> dict:
    streams_of = jax.random.split(jax.random.key(seed), 4)
    volume = scatter_about(streams_of[0], (C, DEPTH, HEIGHT, WIDTH), 1.0, 6.0, ((0, 16), (1, 32)))
    filters = scatter_about(streams_of[1], (F, 3, 3, 3, C), (27 * C) ** -0.5, 0.078125, ((0, 16),))
    cotangent = scatter_about(streams_of[2], (F, DEPTH, HEIGHT, WIDTH), 1.0, 6.0, ((0, 16), (1, 32)))
    return {"volume": volume, "filters": filters, "cotangent": cotangent}


def convolve(field, kernel):
    result = lax.conv_general_dilated(field[None], kernel, (1, 1, 1), ((1, 1), (1, 1), (1, 1)), dimension_numbers=('NCDHW', 'DHWIO', 'NCDHW'), precision=lax.Precision.HIGHEST)
    return result[0]

def reference(volume, filters, cotangent):
    field = volume.astype(jnp.float32)
    kernel = jnp.transpose(filters.astype(jnp.float32), (1, 2, 3, 4, 0))
    response, pullback = jax.vjp(convolve, field, kernel)
    field_grad, kernel_grad = pullback(cotangent.astype(jnp.float32))
    factor = 1.0 / math.sqrt(DEPTH * HEIGHT * WIDTH)
    return (response.astype(jnp.bfloat16), field_grad.astype(jnp.bfloat16), (jnp.transpose(kernel_grad, (4, 0, 1, 2, 3)) * factor).astype(jnp.bfloat16))
```

```python
import math

import jax
import jax.numpy as jnp
from jax import lax
from jax.experimental import pallas as pl
from jax.experimental.pallas import tpu as pltpu
from jax.sharding import Mesh
from jax.sharding import PartitionSpec as P

BF = jnp.bfloat16
F32 = jnp.float32
VMEM = pl.BlockSpec(memory_space=pltpu.VMEM)
SMEM = pl.BlockSpec(memory_space=pltpu.SMEM)
PARAMS = pltpu.CompilerParams(vmem_limit_bytes=48 * 1024 * 1024)


def call(kernel, out_shape, in_specs, scratch=()):
    return pl.pallas_call(
        kernel,
        out_shape=out_shape,
        in_specs=in_specs,
        out_specs=jax.tree.map(lambda _: VMEM, out_shape),
        scratch_shapes=list(scratch),
        compiler_params=PARAMS,
    )


def lane_half(shape):
    return lax.broadcasted_iota(jnp.int32, shape, len(shape) - 1) < 64


def pack_kernel(fil, out):
    low = lane_half((16, 128))
    for r in range(14):
        for half in range(2):
            lanes = pl.ds(128 * half, 128)
            first = fil[2 * r, :, lanes].astype(F32)
            if r < 13:
                second = fil[2 * r + 1, :, lanes].astype(F32)
            else:
                second = jnp.zeros_like(first)
            even = jnp.where(low, first, pltpu.roll(second, 64, 1))
            odd = jnp.where(low, pltpu.roll(first, 64, 1), second)
            out[2 * half, r] = even.astype(BF)
            out[2 * half + 1, r] = odd.astype(BF)


def put(dst, slot, row, block):
    wide = block.astype(F32)
    lane = lax.broadcasted_iota(jnp.int32, (64, 128), 1)
    dst[slot, row, 0] = jnp.where(lane == 0, 0.0, pltpu.roll(wide, 1, 1)).astype(BF)
    dst[slot, row, 1] = block
    dst[slot, row, 2] = jnp.where(lane == 127, 0.0, pltpu.roll(wide, 127, 1)).astype(BF)


def rim(dst, planes):
    zero = jnp.zeros((3, 64, 128), BF)
    for slot in range(planes):
        dst[slot, 0] = zero
        dst[slot, 9] = zero


def window(src, plane, row):
    flat = src[pl.ds(plane, 3), pl.ds(row, 3)].reshape(1728, 128)
    return jnp.concatenate([flat, jnp.zeros((64, 128), BF)], axis=0)


def data_kernel(core, w, own, other, out, planes):
    j = core[0]
    rim(planes, 4)

    def fill(row, _):
        for s in range(3):
            put(planes, s + j, row + 1, own[:, s, row].reshape(64, 128))
        put(planes, 3 * (1 - j), row + 1, other[:, j, row].reshape(64, 128))
        return 0

    lax.fori_loop(0, 8, fill, 0)
    low = lane_half((64, 128))
    row_id = lax.broadcasted_iota(jnp.int32, (64, 128), 0)
    lane_id = lax.broadcasted_iota(jnp.int32, (64, 128), 1)
    pick = jnp.where((lane_id & 63) == row_id, 1.0, 0.0).astype(BF)
    tiles = []
    for r in range(14):
        even = w[:, 13 - r].reshape(64, 128)
        first = jnp.where(low, even.astype(F32), 0.0).astype(BF)
        if r < 13:
            odd = w[:, 12 - r].reshape(64, 128)
            second = jnp.where(low, 0.0, odd.astype(F32)).astype(BF)
        else:
            second = jnp.zeros((64, 128), BF)
        both = jnp.concatenate([first, second], axis=0)
        tiles.append(
            lax.dot_general(
                pick, both, (((1,), (1,)), ((), ())), preferred_element_type=F32
            ).astype(BF)
        )
    lhs = jnp.concatenate(tiles, axis=1)

    def row_pair(step, _):
        p, h = step // 4, 2 * (step % 4)
        rhs = jnp.concatenate([window(planes, p, h), window(planes, p, h + 1)], axis=1)
        res = jnp.dot(lhs, rhs, preferred_element_type=F32)
        out[:, p, h] = res[:, :128].reshape(4, 16, 128)
        out[:, p, h + 1] = res[:, 128:].reshape(4, 16, 128)
        return 0

    lax.fori_loop(0, 8, row_pair, 0)


def volume_kernel(core, w, vown, vother, cown, cother, out, planes, cot, acc):
    j = core[0]
    rim(planes, 6)

    def fill(row, _):
        for s in range(3):
            put(planes, 3 * j + s, row + 1, vown[:, s, row].reshape(64, 128))
            put(planes, 3 * (1 - j) + s, row + 1, vother[:, s, row].reshape(64, 128))
        for s in range(2):
            cot[2 * j + s, row] = cown[:, s + 1 - j, row].reshape(64, 128)
            cot[2 * (1 - j) + s, row] = cother[:, s, row].reshape(64, 128)
        return 0

    lax.fori_loop(0, 8, fill, 0)
    lhs = jnp.concatenate([w[:, r].reshape(64, 128) for r in range(14)], axis=1)

    def row_pair(step, _):
        p, h = step // 4, 2 * (step % 4)
        q = 2 * j + p
        rhs = jnp.concatenate([window(planes, q, h), window(planes, q, h + 1)], axis=1)
        res = jnp.dot(lhs, rhs, preferred_element_type=F32)
        at = (p * 8 + h) * 16
        out[:, pl.ds(at, 16)] = res[:, :128].reshape(4, 16, 128)
        out[:, pl.ds(at + 16, 16)] = res[:, 128:].reshape(4, 16, 128)
        return 0

    lax.fori_loop(0, 8, row_pair, 0)
    acc[...] = jnp.zeros_like(acc)
    half = pl.ds(32 * j, 32)

    def taps(p, h):
        flat = planes[pl.ds(p, 3), pl.ds(h, 3), :, half].reshape(864, 128)
        return jnp.concatenate([flat, jnp.zeros((32, 128), BF)], axis=0)

    def correlate(step, _):
        p, h = step // 4, 2 * (step % 4)
        grad = jnp.concatenate([cot[p, h], cot[p, h + 1]], axis=1)
        rhs = jnp.concatenate([taps(p, h), taps(p, h + 1)], axis=1)
        acc[...] += lax.dot_general(
            grad, rhs, (((1,), (1,)), ((), ())), preferred_element_type=F32
        )
        return 0

    lax.fori_loop(0, 16, correlate, 0)
    for g in range(7):
        out[:, 256 + 16 * g : 272 + 16 * g] = acc[:, 128 * g : 128 * g + 128].reshape(4, 16, 128)
    out[:, 368:384] = jnp.zeros((4, 16, 128), F32)


def place_kernel(core, own, other, out):
    j = core[0]
    lane = lax.broadcasted_iota(jnp.int32, (16, 128), 1) // 32
    for g in range(7):
        blocks = []
        for a in range(4):
            mine = own[a, g].astype(F32)
            theirs = other[a, g].astype(F32)
            blocks.append(jnp.where(j == 0, mine, theirs))
            blocks.append(jnp.where(j == 0, theirs, mine))
        for s in range(4):
            if 4 * g + s >= 27:
                continue
            for side in range(2):
                total = jnp.zeros((16, 128), F32)
                for at in range(4):
                    block = blocks[4 * side + at]
                    turn = (32 * (at - s)) % 128
                    block = pltpu.roll(block, turn, 1) if turn else block
                    total = jnp.where(lane == at, block, total)
                out[4 * g + s, :, 128 * side : 128 * side + 128] = total.astype(BF)


def local(volume, filters, cotangent):
    depth, height, width = volume.shape[1:]
    cells = depth * height * width * lax.axis_size("xz") * lax.axis_size("co")
    core = lax.axis_index("co")
    core_ref = core.reshape(1).astype(jnp.int32)
    chips = lax.axis_size("xz")

    fields = jnp.transpose(jnp.stack([volume, cotangent]), (0, 2, 3, 1, 4))
    outer = jnp.where(core == 0, fields[:, 0], fields[:, 1])
    links = [(2 * i + 1, 2 * i + 2) for i in range(chips - 1)]
    links = links + [(t, s) for s, t in links]
    rims = lax.ppermute(outer, ("xz", "co"), links)[:, None]
    fields = jnp.where(
        core == 0,
        jnp.concatenate([rims, fields], axis=1),
        jnp.concatenate([fields, rims], axis=1),
    )

    packed = call(pack_kernel, jax.ShapeDtypeStruct((4, 14, 16, 128), BF), [VMEM])(
        jnp.transpose(filters, (1, 2, 3, 0, 4)).reshape(27, 16, 256)
    )
    to_a = jnp.concatenate(
        [
            jnp.broadcast_to(fields[1].reshape(1, 384, 128), (4, 384, 128)),
            packed.reshape(4, 224, 128),
        ],
        axis=1,
    )
    from_a = lax.all_to_all(to_a, "a", 0, 0)
    grad = from_a[:, :384].reshape(4, 3, 8, 16, 128)
    weights = from_a[:, 384:].reshape(4, 14, 16, 128)
    vol = lax.all_to_all(jnp.broadcast_to(fields[:1], (4, 3, 8, 16, 128)), "b", 0, 0)

    swap = [(0, 1), (1, 0)]
    grad_own = jnp.where(core == 0, grad[:, 1:], grad[:, :2])
    grad_other = lax.ppermute(grad_own, "co", swap)
    vol_other = lax.ppermute(vol, "co", swap)

    data = call(
        data_kernel,
        jax.ShapeDtypeStruct((4, 2, 8, 16, 128), F32),
        [SMEM, VMEM, VMEM, VMEM],
        [pltpu.VMEM((4, 10, 3, 64, 128), BF)],
    )(core_ref, weights, grad, grad_other)
    parts = call(
        volume_kernel,
        jax.ShapeDtypeStruct((4, 384, 128), F32),
        [SMEM, VMEM, VMEM, VMEM, VMEM, VMEM],
        [
            pltpu.VMEM((6, 10, 3, 64, 128), BF),
            pltpu.VMEM((4, 8, 64, 128), BF),
            pltpu.VMEM((64, 896), F32),
        ],
    )(core_ref, weights, vol, vol_other, grad, grad_other)

    parts = lax.all_to_all(parts, "a", 0, 0)
    data = lax.all_to_all(data, "b", 0, 0)
    response = jnp.sum(parts[:, :256].reshape(4, 2, 8, 16, 128), axis=0)
    kernel = lax.all_to_all(parts[:, 256:].reshape(16, 32, 128), "xz", 0, 0)
    factor = 1.0 / math.sqrt(cells)
    kernel = (jnp.sum(kernel, axis=0) * factor).astype(BF)
    kernel = lax.all_to_all(jnp.broadcast_to(kernel[None], (16, 32, 128)), "xz", 0, 0)
    kernel = kernel.reshape(4, 8, 16, 128)
    kernel_other = lax.ppermute(kernel, "co", swap)
    placed = call(place_kernel, jax.ShapeDtypeStruct((27, 16, 256), BF), [SMEM, VMEM, VMEM])(
        core_ref, kernel, kernel_other
    )
    order = (2, 0, 1, 3)
    return (
        jnp.transpose(response.astype(BF), order),
        jnp.transpose(jnp.sum(data, axis=0).astype(BF), order),
        jnp.transpose(placed.reshape(3, 3, 3, 16, 256), (3, 0, 1, 2, 4)),
    )


def solution(mesh):
    grid = Mesh(mesh.devices.reshape(16, 2, 4, 4), ("xz", "co", "a", "b"))
    cells = P(("a", "b"), ("xz", "co"), None, None)
    kernel = P(("a", "b"), None, None, None, None)
    return jax.shard_map(
        local,
        mesh=grid,
        in_specs=(cells, kernel, cells),
        out_specs=(cells, cells, kernel),
        check_vma=False,
    )
```

```python
import math

import jax
import jax.numpy as jnp
from jax import lax
from jax.experimental import pallas as pl
from jax.experimental.pallas import tpu as pltpu
from jax.sharding import Mesh
from jax.sharding import PartitionSpec as P

BF = jnp.bfloat16
F32 = jnp.float32
F16 = jnp.float16
VMEM = pl.BlockSpec(memory_space=pltpu.VMEM)
SMEM = pl.BlockSpec(memory_space=pltpu.SMEM)
PARAMS = pltpu.CompilerParams(vmem_limit_bytes=48 * 1024 * 1024)
NT = (((1,), (1,)), ((), ()))


def call(kernel, out_shape, operands, scratch=(), micros=1):
    return pl.pallas_call(
        kernel,
        out_shape=out_shape,
        in_specs=[SMEM] + [VMEM] * (len(operands) - 1),
        out_specs=jax.tree.map(lambda _: VMEM, out_shape),
        scratch_shapes=list(scratch),
        compiler_params=PARAMS,
        cost_estimate=pl.CostEstimate(
            flops=int(micros * 1e9), bytes_accessed=1 << 18, transcendentals=0
        ),
    )(*operands)


def iota(shape, dim):
    return lax.broadcasted_iota(jnp.int32, shape, dim)


def size_of(peak):
    most = jnp.max(jnp.max(peak, axis=0, keepdims=True), axis=1, keepdims=True)
    power = jnp.floor(jnp.log2(jnp.clip(most, 2.0**-100, 2.0**100)))
    return jnp.broadcast_to(power, (8, 128))


def pack_kernel(place, fil, own, send):
    zh = place[2]
    lane = iota((256, 256), 1)
    wanted = (lane % 128) // 16 * 32 + (zh ^ (lane // 128)) * 16 + lane % 16
    pick = jnp.where(iota((256, 256), 0) == wanted, 1.0, 0.0).astype(BF)
    res = jnp.dot(fil[...].reshape(432, 256), pick, preferred_element_type=F32).astype(BF)
    own[...] = res[:, :128].reshape(27, 16, 128)
    send[...] = res[:, 128:].reshape(27, 16, 128)


def put(dst, slot, row, block):
    wide = block.astype(F32)
    lane = iota(block.shape, 1)
    dst[slot, row, 0] = jnp.where(lane == 0, 0.0, pltpu.roll(wide, 1, 1)).astype(BF)
    dst[slot, row, 1] = block
    dst[slot, row, 2] = jnp.where(lane == 127, 0.0, pltpu.roll(wide, 127, 1)).astype(BF)


def data_kernel(place, wown, wgot, own, got, other, rim, out, power, planes, peak):
    j = place[0]
    zero = jnp.zeros((3, 32, 128), BF)
    for slot in range(4):
        planes[slot, 0] = zero
        planes[slot, 9] = zero

    def fill(row, _):
        for s in range(2):
            put(planes, 1 + s, row + 1, jnp.concatenate([own[s, row], got[s, row]], axis=0))
        near = jnp.concatenate([other[0, j, row], other[1, j, row]], axis=0)
        put(planes, 3 * (1 - j), row + 1, near)
        put(planes, 3 * j, row + 1, jnp.concatenate([rim[0, row], rim[1, row]], axis=0))
        return 0

    lax.fori_loop(0, 8, fill, 0)
    peak[...] = jnp.zeros_like(peak)
    same = jnp.where(iota((128, 128), 0) == iota((128, 128), 1), 1.0, 0.0).astype(BF)
    tiles = []
    for g in range(7):
        rows = []
        for s in range(4):
            t = 26 - 4 * g - s
            rows += [wown[t], wgot[t]] if t >= 0 else [jnp.zeros((32, 128), BF)]
        tile = lax.dot_general(
            same, jnp.concatenate(rows, axis=0), NT, preferred_element_type=F32
        )
        tiles.append(tile.astype(BF))
    lhs = jnp.concatenate(tiles, axis=1)

    def window(plane, row):
        flat = planes[pl.ds(plane, 3), pl.ds(row, 3)].reshape(864, 128)
        return jnp.concatenate([flat, jnp.zeros((32, 128), BF)], axis=0)

    def row_pair(step, _):
        p, h = step // 4, 2 * (step % 4)
        rhs = jnp.concatenate([window(p, h), window(p, h + 1)], axis=1)
        res = jnp.dot(lhs, rhs, preferred_element_type=F32)
        at = (p * 8 + h) * 16
        out[:, pl.ds(at, 16)] = res[:, :128].reshape(8, 16, 128)
        out[:, pl.ds(at + 16, 16)] = res[:, 128:].reshape(8, 16, 128)
        sizes = jnp.maximum(jnp.abs(res[:, :128]), jnp.abs(res[:, 128:]))
        peak[...] = jnp.maximum(peak[...], jnp.max(sizes.reshape(16, 8, 128), axis=0))
        return 0

    lax.fori_loop(0, 8, row_pair, 0)
    size = size_of(peak[...])
    power[:8] = size
    power[8:] = size


def volume_kernel(
    place, wown, wgot, vown, vother, cown, cgot, cother, keep, send, power, planes, cot, resp, acc
):
    j = place[0]
    cot[...] = jnp.zeros_like(cot)
    resp[...] = jnp.zeros_like(resp)
    half = pl.ds(pl.multiple_of(64 * j, 64), 64)

    def fill(row, _):
        for s in range(3):
            put(planes, 3 * j + s, row, vown[:, s, row].reshape(128, 128))
            put(planes, 3 * (1 - j) + s, row, vother[:, s, row].reshape(128, 128))
        for s in range(2):
            cot[2 + 2 * j + s, row + 1] = jnp.concatenate([cown[s, row], cgot[s, row]], axis=0)
            cot[4 - 2 * j + s, row + 1] = jnp.concatenate(
                [cother[0, s, row], cother[1, s, row]], axis=0
            )
        return 0

    lax.fori_loop(0, 8, fill, 0)

    weights = jnp.concatenate(
        [
            jnp.concatenate(
                [jnp.concatenate([wown[3 * ab + c], wgot[3 * ab + c]], axis=0) for c in range(3)],
                axis=1,
            )
            for ab in range(9)
        ],
        axis=0,
    )

    def row_pair(step, _):
        h = 2 * step
        for q in range(4):
            taps = [a for a in range(3) if 0 <= q - a < 2]
            lhs = weights[96 * taps[0] : 96 * taps[-1] + 96]
            first = planes[2 * j + q, h].reshape(384, 128)
            second = planes[2 * j + q, h + 1].reshape(384, 128)
            res = jnp.dot(
                lhs, jnp.concatenate([first, second], axis=1), preferred_element_type=F32
            )
            for n, a in enumerate(taps):
                for b in range(3):
                    at = 96 * n + 32 * b
                    resp[q - a, h + 2 - b] += res[at : at + 32, :128]
                    resp[q - a, h + 3 - b] += res[at : at + 32, 128:]
        return 0

    lax.fori_loop(0, 4, row_pair, 0)
    peak = jnp.zeros((8, 128), F32)
    for p in range(2):
        for h in range(8):
            at = (p * 8 + h) * 16
            keep[at : at + 16] = resp[p, h + 1, :16]
            part = resp[p, h + 1, 16:]
            send[at : at + 16] = part
            peak = jnp.maximum(peak, jnp.max(jnp.abs(part).reshape(2, 8, 128), axis=0))
    power[:8] = size_of(peak)

    acc[...] = jnp.zeros_like(acc)
    for q in range(6):
        low, high = max(0, 2 - q), min(2, 5 - q)
        lhs, rhs = [], []
        for h in range(8):
            grads = cot[q + low : q + high + 1, h : h + 3]
            lhs.append(grads.reshape(96 * (high - low + 1), 128))
            taps = planes[q, h, :, half].reshape(192, 128)
            rhs.append(jnp.concatenate([taps, jnp.zeros((64, 128), BF)], axis=0))
        res = lax.dot_general(
            jnp.concatenate(lhs, axis=1),
            jnp.concatenate(rhs, axis=1),
            NT,
            preferred_element_type=F32,
        )
        acc[96 * low : 96 * high + 96] += res
    for side, out in enumerate((keep, send)):
        third = []
        for ab in range(9):
            rows = pl.ds(32 * ab + 16 * side, 16)
            out[256 + 16 * ab : 272 + 16 * ab] = acc[rows, :128]
            third.append(acc[rows, 128:])
        for n in range(5):
            tile = third[2 * n]
            if n < 4:
                tile = tile + pltpu.roll(third[2 * n + 1], 64, 1)
            out[400 + 16 * n : 416 + 16 * n] = tile
        out[480:512] = jnp.zeros((32, 128), F32)
    peak = jnp.max(jnp.abs(send[256:480]).reshape(28, 8, 128), axis=0)
    power[8:] = size_of(peak)


def place_kernel(place, own, other, out):
    j, zh = place[0], place[2]
    lane, n = iota((128, 512), 0), iota((128, 512), 1)
    y, z, i, s = n % 256 // 32, n % 32 // 16, n % 16, n // 256
    source = s * 64 + y % 4 * 16 + i
    total = jnp.zeros((224, 512), F32)
    for core, ref in enumerate((own, other)):
        for turn in range(2):
            hit = (lane == source) & (y // 4 == (j ^ core)) & ((z ^ zh) == turn)
            pick = jnp.where(hit, 1.0, 0.0).astype(BF)
            part = ref[turn, :14].reshape(224, 128)
            total = total + jnp.dot(part, pick, preferred_element_type=F32)
    for r in range(14):
        for s in range(2):
            ab, c = (r, s) if r < 9 else (2 * (r - 9) + s, 2)
            if ab > 8:
                continue
            t = (2 - ab // 3) * 9 + (2 - ab % 3) * 3 + c
            out[t] = total[16 * r : 16 * r + 16, 256 * s : 256 * s + 256].astype(BF)


def shrink(value, power):
    return (value * jnp.exp2(14.0 - power)).astype(F16)


def grow(value, power):
    return value.astype(F32) * jnp.exp2(power.astype(F32) - 14.0)


def local(volume, filters, cotangent):
    depth, height, width = volume.shape[1:]
    cells = depth * height * width * lax.axis_size("xz") * lax.axis_size("co")
    chips = lax.axis_size("xz")
    core = lax.axis_index("co")
    place = jnp.stack([core, lax.axis_index("y"), lax.axis_index("zh")]).astype(jnp.int32)
    swap = [(0, 1), (1, 0)]

    fields = jnp.transpose(jnp.stack([volume, cotangent]), (0, 2, 3, 1, 4))
    grad = fields[1]
    near = [(2 * i + 1, 2 * i + 2) for i in range(chips - 1)]
    near = near + [(t, s) for s, t in near]

    def rim_of(value, axis):
        return lax.dynamic_index_in_dim(value, core, axis, keepdims=False)

    tap_blocks = jnp.transpose(filters, (1, 2, 3, 0, 4)).reshape(27, 16, 256)
    wown, wsend = call(
        pack_kernel, [jax.ShapeDtypeStruct((27, 16, 128), BF)] * 2, [place, tap_blocks]
    )
    pair = lax.ppermute(
        jnp.concatenate([grad.reshape(256, 128), wsend.reshape(432, 128)]), "zh", swap
    )
    grad_got = pair[:256].reshape(2, 8, 16, 128)
    wgot = pair[256:].reshape(27, 16, 128)
    both = jnp.stack([grad, grad_got])
    grad_other = lax.ppermute(both, "co", swap)
    grad_rim = lax.ppermute(rim_of(both, 1), ("xz", "co"), near)

    data, size = call(
        data_kernel,
        [jax.ShapeDtypeStruct((8, 256, 128), F32), jax.ShapeDtypeStruct((16, 128), F32)],
        [place, wown, wgot, grad, grad_got, grad_other, grad_rim],
        [pltpu.VMEM((4, 10, 3, 32, 128), BF), pltpu.VMEM((8, 128), F32)],
        micros=6,
    )
    data = jnp.concatenate(
        [shrink(data, size[0, 0]), jnp.broadcast_to(size[None].astype(F16), (8, 16, 128))], axis=1
    )
    rim = lax.ppermute(rim_of(fields[0], 0), ("xz", "co"), near)[None]
    slab = jnp.where(
        core == 0,
        jnp.concatenate([rim, fields[0]], axis=0),
        jnp.concatenate([fields[0], rim], axis=0),
    )
    vol = lax.all_to_all(jnp.broadcast_to(slab[None], (8, 3, 8, 16, 128)), "y", 0, 0)
    vol, data = lax.optimization_barrier((vol, data))
    vol_other = lax.ppermute(vol, "co", swap)
    keep, send, size = call(
        volume_kernel,
        [jax.ShapeDtypeStruct((512, 128), F32)] * 2 + [jax.ShapeDtypeStruct((16, 128), F32)],
        [place, wown, wgot, vol, vol_other, grad, grad_got, grad_other],
        [
            pltpu.VMEM((6, 8, 3, 128, 128), BF),
            pltpu.VMEM((8, 10, 32, 128), BF),
            pltpu.VMEM((2, 10, 32, 128), F32),
            pltpu.VMEM((288, 256), F32),
        ],
        micros=8,
    )
    send = jnp.concatenate(
        [shrink(send[:256], size[0, 0]), shrink(send[256:], size[8, 0]), size.astype(F16)]
    )
    got = lax.ppermute(send, "zh", swap)
    data = lax.all_to_all(data, "y", 0, 0)
    keep, got, data = lax.optimization_barrier((keep, got, data))

    kernel = jnp.concatenate([keep[256:], grow(got[256:512], got[520, 0])]).reshape(16, 32, 128)
    kernel = lax.all_to_all(kernel, "xz", 0, 0)
    factor = 1.0 / math.sqrt(cells)
    kernel = (jnp.sum(kernel, axis=0) * factor).astype(BF)
    kernel = lax.all_to_all(jnp.broadcast_to(kernel[None], (16, 32, 128)), "xz", 0, 0)
    kernel = kernel.reshape(2, 16, 16, 128)
    kernel_other = lax.ppermute(kernel, "co", swap)
    placed = call(
        place_kernel, jax.ShapeDtypeStruct((27, 16, 256), BF), [place, kernel, kernel_other]
    )
    order = (2, 0, 1, 3)
    response = (keep[:256] + grow(got[:256], got[512, 0])).reshape(2, 8, 16, 128)
    data = jnp.sum(grow(data[:, :256], data[:, 256:257, :1]), axis=0).reshape(2, 8, 16, 128)
    return (
        jnp.transpose(response.astype(BF), order),
        jnp.transpose(data.astype(BF), order),
        jnp.transpose(placed.reshape(3, 3, 3, 16, 256), (3, 0, 1, 2, 4)),
    )


def solution(mesh):
    grid = Mesh(mesh.devices.reshape(16, 2, 8, 2), ("xz", "co", "y", "zh"))
    cells = P(("y", "zh"), ("xz", "co"), None, None)
    kernel = P(("y", "zh"), None, None, None, None)
    return jax.shard_map(
        local,
        mesh=grid,
        in_specs=(cells, kernel, cells),
        out_specs=(cells, cells, kernel),
        check_vma=False,
    )
```

```python
import functools
import math

import jax
import jax.numpy as jnp
from jax import lax
from jax.experimental import pallas as pl
from jax.experimental.pallas import tpu as pltpu
from jax.sharding import Mesh
from jax.sharding import PartitionSpec as P

BF = jnp.bfloat16
F32 = jnp.float32
F16 = jnp.float16
VMEM = pl.BlockSpec(memory_space=pltpu.VMEM)
SMEM = pl.BlockSpec(memory_space=pltpu.SMEM)
PARAMS = pltpu.CompilerParams(vmem_limit_bytes=48 * 1024 * 1024)
NT = (((1,), (1,)), ((), ()))


def call(kernel, out_shape, operands, scratch=(), micros=1):
    return pl.pallas_call(
        kernel,
        out_shape=out_shape,
        in_specs=[SMEM] + [VMEM] * (len(operands) - 1),
        out_specs=jax.tree.map(lambda _: VMEM, out_shape),
        scratch_shapes=list(scratch),
        compiler_params=PARAMS,
        cost_estimate=pl.CostEstimate(
            flops=int(micros * 1e9), bytes_accessed=1 << 18, transcendentals=0
        ),
    )(*operands)


def iota(shape, dim):
    return lax.broadcasted_iota(jnp.int32, shape, dim)


def size_of(peak):
    most = jnp.max(jnp.max(peak, axis=0, keepdims=True), axis=1, keepdims=True)
    power = jnp.floor(jnp.log2(jnp.clip(most, 2.0**-100, 2.0**100)))
    return jnp.broadcast_to(power, (8, 128))


def pack_kernel(place, fil, own, send):
    zh = place[2]
    lane = iota((256, 256), 1)
    wanted = (lane % 128) // 16 * 32 + (zh ^ (lane // 128)) * 16 + lane % 16
    pick = jnp.where(iota((256, 256), 0) == wanted, 1.0, 0.0).astype(BF)
    res = jnp.dot(fil[...].reshape(432, 256), pick, preferred_element_type=F32).astype(BF)
    own[...] = res[:, :128].reshape(27, 16, 128)
    send[...] = res[:, 128:].reshape(27, 16, 128)


def put(dst, slot, row, block):
    wide = block.astype(F32)
    lane = iota(block.shape, 1)
    dst[slot, row, 0] = jnp.where(lane == 0, 0.0, pltpu.roll(wide, 1, 1)).astype(BF)
    dst[slot, row, 1] = block
    dst[slot, row, 2] = jnp.where(lane == 127, 0.0, pltpu.roll(wide, 127, 1)).astype(BF)


def data_kernel(place, wown, wgot, own, got, other, rim, keep, send, planes, peak):
    j = place[0]
    zero = jnp.zeros((3, 32, 128), BF)
    for slot in range(4):
        planes[slot, 0] = zero
        planes[slot, 9] = zero

    def fill(row, _):
        for s in range(2):
            put(planes, 1 + s, row + 1, jnp.concatenate([own[s, row], got[s, row]], axis=0))
        near = jnp.concatenate([other[0, j, row], other[1, j, row]], axis=0)
        put(planes, 3 * (1 - j), row + 1, near)
        put(planes, 3 * j, row + 1, jnp.concatenate([rim[0, row], rim[1, row]], axis=0))
        return 0

    lax.fori_loop(0, 8, fill, 0)
    peak[...] = jnp.zeros_like(peak)
    turned = iota((128, 128), 0) ^ (16 * place[1])
    pick = jnp.where(turned == iota((128, 128), 1), 1.0, 0.0).astype(BF)
    tiles = []
    for g in range(7):
        rows = []
        for s in range(4):
            t = 26 - 4 * g - s
            rows += [wown[t], wgot[t]] if t >= 0 else [jnp.zeros((32, 128), BF)]
        tile = lax.dot_general(
            pick, jnp.concatenate(rows, axis=0), NT, preferred_element_type=F32
        )
        tiles.append(tile.astype(BF))
    lhs = jnp.concatenate(tiles, axis=1)

    def window(plane, row):
        flat = planes[pl.ds(plane, 3), pl.ds(row, 3)].reshape(864, 128)
        return jnp.concatenate([flat, jnp.zeros((32, 128), BF)], axis=0)

    def row_pair(step, _):
        p, h = step // 4, 2 * (step % 4)
        rhs = jnp.concatenate([window(p, h), window(p, h + 1)], axis=1)
        res = jnp.dot(lhs, rhs, preferred_element_type=F32)
        at = (p * 8 + h) * 16
        for m in range(8):
            out = send if m % 2 else keep
            rows = pl.ds(m // 2 * 256 + at, 16)
            out[rows] = res[16 * m : 16 * m + 16, :128]
            rows = pl.ds(m // 2 * 256 + at + 16, 16)
            out[rows] = res[16 * m : 16 * m + 16, 128:]
        sizes = jnp.maximum(jnp.abs(res[:, :128]), jnp.abs(res[:, 128:]))
        peak[...] = jnp.maximum(peak[...], jnp.max(sizes.reshape(16, 8, 128), axis=0))
        return 0

    lax.fori_loop(0, 8, row_pair, 0)
    size = size_of(peak[...])
    scale = jnp.exp2(14.0 - size)

    def bring(step, _):
        rows = pl.ds(pl.multiple_of(step * 64, 64), 64)
        send[rows] = (send[rows].reshape(8, 8, 128) * scale).reshape(64, 128)
        return 0

    lax.fori_loop(0, 16, bring, 0)
    send[1024:1032] = size
    send[1032:1040] = size


def volume_kernel(
    place, wown, wgot, vown, vother, cown, cgot, cother, rkeep, rsend, taps, planes, cot, resp, acc
):
    j = place[0]
    cot[...] = jnp.zeros_like(cot)
    resp[...] = jnp.zeros_like(resp)
    half = pl.ds(pl.multiple_of(64 * j, 64), 64)

    def fill(row, _):
        for s in range(3):
            put(planes, 3 * j + s, row, vown[:, s, row].reshape(128, 128))
            put(planes, 3 * (1 - j) + s, row, vother[:, s, row].reshape(128, 128))
        for s in range(2):
            cot[2 + 2 * j + s, row + 1] = jnp.concatenate([cown[s, row], cgot[s, row]], axis=0)
            cot[4 - 2 * j + s, row + 1] = jnp.concatenate(
                [cother[0, s, row], cother[1, s, row]], axis=0
            )
        return 0

    lax.fori_loop(0, 8, fill, 0)

    weights = jnp.concatenate(
        [
            jnp.concatenate(
                [jnp.concatenate([wown[3 * ab + c], wgot[3 * ab + c]], axis=0) for c in range(3)],
                axis=1,
            )
            for ab in range(9)
        ],
        axis=0,
    )

    def row_pair(step, _):
        h = 2 * step
        for q in range(4):
            reach = [a for a in range(3) if 0 <= q - a < 2]
            lhs = weights[96 * reach[0] : 96 * reach[-1] + 96]
            first = planes[2 * j + q, h].reshape(384, 128)
            second = planes[2 * j + q, h + 1].reshape(384, 128)
            res = jnp.dot(
                lhs, jnp.concatenate([first, second], axis=1), preferred_element_type=F32
            )
            for n, a in enumerate(reach):
                for b in range(3):
                    at = 96 * n + 32 * b
                    resp[q - a, h + 2 - b] += res[at : at + 32, :128]
                    resp[q - a, h + 3 - b] += res[at : at + 32, 128:]
        return 0

    lax.fori_loop(0, 4, row_pair, 0)
    peak = jnp.zeros((8, 128), F32)
    for p in range(2):
        for h in range(8):
            at = (p * 8 + h) * 16
            rkeep[at : at + 16] = resp[p, h + 1, :16]
            part = resp[p, h + 1, 16:]
            peak = jnp.maximum(peak, jnp.max(jnp.abs(part).reshape(2, 8, 128), axis=0))
    size = size_of(peak)
    scale = jnp.exp2(14.0 - size)
    for p in range(2):
        for h in range(8):
            at = (p * 8 + h) * 16
            part = resp[p, h + 1, 16:].reshape(2, 8, 128) * scale
            rsend[at : at + 16] = part.reshape(16, 128)
    rsend[256:264] = size
    rsend[264:272] = size

    acc[...] = jnp.zeros_like(acc)
    for q in range(6):
        low, high = max(0, 2 - q), min(2, 5 - q)
        lhs, rhs = [], []
        for h in range(8):
            grads = cot[q + low : q + high + 1, h : h + 3]
            lhs.append(grads.reshape(96 * (high - low + 1), 128))
            shifted = planes[q, h, :, half].reshape(192, 128)
            rhs.append(jnp.concatenate([shifted, jnp.zeros((64, 128), BF)], axis=0))
        res = lax.dot_general(
            jnp.concatenate(lhs, axis=1),
            jnp.concatenate(rhs, axis=1),
            NT,
            preferred_element_type=F32,
        )
        acc[96 * low : 96 * high + 96] += res
    for side in range(2):
        tiles, third = [], []
        for ab in range(9):
            rows = pl.ds(32 * ab + 16 * side, 16)
            tiles.append(acc[rows, :128])
            third.append(acc[rows, 128:])
        for n in range(4):
            tiles.append(third[2 * n] + pltpu.roll(third[2 * n + 1], 64, 1))
        tiles.append(third[8])
        for r, tile in enumerate(tiles):
            at = 32 * r + 16 * side
            taps[at : at + 16] = tile
    taps[448:512] = jnp.zeros((64, 128), F32)


def sum_kernel(factor, place, parts, out):
    total = parts[0]
    for n in range(1, 16):
        total = total + parts[n]
    out[...] = (total * factor).astype(BF)


def place_kernel(place, own, other, out):
    j = place[0]
    lane, n = iota((128, 512), 0), iota((128, 512), 1)
    y, z, i, s = n % 256 // 32, n % 32 // 16, n % 16, n // 256
    source = s * 64 + y % 4 * 16 + i
    total = jnp.zeros((224, 512), F32)
    for core, ref in enumerate((own, other)):
        for side in range(2):
            hit = (lane == source) & (y // 4 == (j ^ core)) & (z == side)
            pick = jnp.where(hit, 1.0, 0.0).astype(BF)
            part = ref[:14, side].reshape(224, 128)
            total = total + jnp.dot(part, pick, preferred_element_type=F32)
    for r in range(14):
        for s in range(2):
            ab, c = (r, s) if r < 9 else (2 * (r - 9) + s, 2)
            if ab > 8:
                continue
            t = (2 - ab // 3) * 9 + (2 - ab % 3) * 3 + c
            out[t] = total[16 * r : 16 * r + 16, 256 * s : 256 * s + 256].astype(BF)


def grow(value, power):
    return value.astype(F32) * jnp.exp2(power.astype(F32) - 14.0)


def split(total, power):
    count = total.shape[0] // 2
    send = (total[1::2] * jnp.exp2(14.0 - power)).reshape(count * 256, 128)
    return total[::2], jnp.concatenate([send, jnp.broadcast_to(power, (16, 128))])


def exchange(total, send, turn):
    got = lax.ppermute(send.astype(F16), "y", [(i, i ^ turn) for i in range(8)])
    return merge(total, send, got)


def merge(total, send, got):
    count = total.shape[0]
    theirs = got[256 * count : 256 * count + 1]
    total = total + grow(got[: 256 * count], theirs).reshape(count, 256, 128)
    return total, jnp.maximum(send[256 * count : 256 * count + 1], theirs.astype(F32)) + 1.0


def local(volume, filters, cotangent):
    depth, height, width = volume.shape[1:]
    cells = depth * height * width * lax.axis_size("xz") * lax.axis_size("co")
    chips = lax.axis_size("xz")
    core = lax.axis_index("co")
    place = jnp.stack([core, lax.axis_index("y"), lax.axis_index("zh")]).astype(jnp.int32)
    swap = [(0, 1), (1, 0)]

    fields = jnp.transpose(jnp.stack([volume, cotangent]), (0, 2, 3, 1, 4))
    grad = fields[1]
    near = [(2 * i + 1, 2 * i + 2) for i in range(chips - 1)]
    near = near + [(t, s) for s, t in near]

    def rim_of(value, axis):
        return lax.dynamic_index_in_dim(value, core, axis, keepdims=False)

    tap_blocks = jnp.transpose(filters, (1, 2, 3, 0, 4)).reshape(27, 16, 256)
    wown, wsend = call(
        pack_kernel, [jax.ShapeDtypeStruct((27, 16, 128), BF)] * 2, [place, tap_blocks]
    )
    pair = lax.ppermute(
        jnp.concatenate([grad.reshape(256, 128), wsend.reshape(432, 128)]), "zh", swap
    )
    grad_got = pair[:256].reshape(2, 8, 16, 128)
    wgot = pair[256:].reshape(27, 16, 128)
    both = jnp.stack([grad, grad_got])
    grad_other = lax.ppermute(both, "co", swap)
    grad_rim = lax.ppermute(rim_of(both, 1), ("xz", "co"), near)

    data_keep, data_send = call(
        data_kernel,
        [jax.ShapeDtypeStruct((1024, 128), F32), jax.ShapeDtypeStruct((1040, 128), F32)],
        [place, wown, wgot, grad, grad_got, grad_other, grad_rim],
        [pltpu.VMEM((4, 10, 3, 32, 128), BF), pltpu.VMEM((8, 128), F32)],
        micros=10,
    )
    rim = lax.ppermute(rim_of(fields[0], 0), ("xz", "co"), near)[None]
    slab = jnp.where(
        core == 0,
        jnp.concatenate([rim, fields[0]], axis=0),
        jnp.concatenate([fields[0], rim], axis=0),
    )
    vol = lax.all_to_all(jnp.broadcast_to(slab[None], (8, 3, 8, 16, 128)), "y", 0, 0)
    vol, data_keep, data_send = lax.optimization_barrier((vol, data_keep, data_send))
    vol_other = lax.ppermute(vol, "co", swap)
    data_got = lax.ppermute(data_send.astype(F16), "y", [(i, i ^ 1) for i in range(8)])
    rkeep, rsend, taps = call(
        volume_kernel,
        [jax.ShapeDtypeStruct((rows, 128), F32) for rows in (256, 272, 512)],
        [place, wown, wgot, vol, vol_other, grad, grad_got, grad_other],
        [
            pltpu.VMEM((6, 8, 3, 128, 128), BF),
            pltpu.VMEM((8, 10, 32, 128), BF),
            pltpu.VMEM((2, 10, 32, 128), F32),
            pltpu.VMEM((288, 256), F32),
        ],
        micros=8,
    )
    kernel = lax.all_to_all(taps.reshape(16, 32, 128), "xz", 0, 0)
    got = lax.ppermute(rsend.astype(F16), "zh", swap)

    kernel, data_got1 = lax.optimization_barrier((kernel, data_got))
    kernel = call(
        functools.partial(sum_kernel, 1.0 / math.sqrt(cells)),
        jax.ShapeDtypeStruct((32, 128), BF),
        [place, kernel],
    )
    data, power = merge(data_keep.reshape(4, 256, 128), data_send, data_got1)
    data, power = exchange(*split(data, power), 2)
    data_keep, data_send = split(data, power)
    data_got = lax.ppermute(data_send.astype(F16), "y", [(i, i ^ 4) for i in range(8)])

    halves = kernel.reshape(2, 16, 128)
    halves = jnp.where(lax.axis_index("zh") == 0, halves, halves[::-1])
    kernel = jnp.broadcast_to(halves[None], (16, 2, 16, 128)).reshape(32, 16, 128)
    kernel = lax.all_to_all(kernel, ("xz", "zh"), 0, 0).reshape(16, 2, 16, 128)
    kernel, got = lax.optimization_barrier((kernel, got))
    response = (rkeep + grow(got[:256], got[256:257])).reshape(2, 8, 16, 128)
    kernel_other = lax.ppermute(kernel, "co", swap)
    kernel_other, data_got = lax.optimization_barrier((kernel_other, data_got))
    data, power = merge(data_keep, data_send, data_got)
    data = data.reshape(2, 8, 16, 128)
    placed = call(
        place_kernel, jax.ShapeDtypeStruct((27, 16, 256), BF), [place, kernel, kernel_other]
    )
    order = (2, 0, 1, 3)
    return (
        jnp.transpose(response.astype(BF), order),
        jnp.transpose(data.astype(BF), order),
        jnp.transpose(placed.reshape(3, 3, 3, 16, 256), (3, 0, 1, 2, 4)),
    )


def solution(mesh):
    grid = Mesh(mesh.devices.reshape(16, 2, 8, 2), ("xz", "co", "y", "zh"))
    cells = P(("y", "zh"), ("xz", "co"), None, None)
    kernel = P(("y", "zh"), None, None, None, None)
    return jax.shard_map(
        local,
        mesh=grid,
        in_specs=(cells, kernel, cells),
        out_specs=(cells, cells, kernel),
        check_vma=False,
    )
```

```python
import functools
import math

import jax
import jax.numpy as jnp
from jax import lax
from jax.experimental import pallas as pl
from jax.experimental.pallas import tpu as pltpu
from jax.sharding import Mesh
from jax.sharding import PartitionSpec as P

BF = jnp.bfloat16
F32 = jnp.float32
F16 = jnp.float16
VMEM = pl.BlockSpec(memory_space=pltpu.VMEM)
SMEM = pl.BlockSpec(memory_space=pltpu.SMEM)
PARAMS = pltpu.CompilerParams(vmem_limit_bytes=48 * 1024 * 1024)
NT = (((1,), (1,)), ((), ()))


def call(kernel, out_shape, operands, scratch=(), micros=1):
    return pl.pallas_call(
        kernel,
        out_shape=out_shape,
        in_specs=[SMEM] + [VMEM] * (len(operands) - 1),
        out_specs=jax.tree.map(lambda _: VMEM, out_shape),
        scratch_shapes=list(scratch),
        compiler_params=PARAMS,
        cost_estimate=pl.CostEstimate(
            flops=int(micros * 1e9), bytes_accessed=1 << 18, transcendentals=0
        ),
    )(*operands)


def iota(shape, dim):
    return lax.broadcasted_iota(jnp.int32, shape, dim)


def size_of(peak):
    most = jnp.max(jnp.max(peak, axis=0, keepdims=True), axis=1, keepdims=True)
    power = jnp.floor(jnp.log2(jnp.clip(most, 2.0**-100, 2.0**100)))
    return jnp.broadcast_to(power, (8, 128))


def pack_kernel(place, fil, own, send):
    zh = place[2]
    lane = iota((256, 256), 1)
    wanted = (lane % 128) // 16 * 32 + (zh ^ (lane // 128)) * 16 + lane % 16
    pick = jnp.where(iota((256, 256), 0) == wanted, 1.0, 0.0).astype(BF)
    res = jnp.dot(fil[...].reshape(432, 256), pick, preferred_element_type=F32).astype(BF)
    own[...] = res[:, :128].reshape(27, 16, 128)
    send[...] = res[:, 128:].reshape(27, 16, 128)


def put(dst, slot, row, block):
    wide = block.astype(F32)
    lane = iota(block.shape, 1)
    dst[slot, row, 0] = jnp.where(lane == 0, 0.0, pltpu.roll(wide, 1, 1)).astype(BF)
    dst[slot, row, 1] = block
    dst[slot, row, 2] = jnp.where(lane == 127, 0.0, pltpu.roll(wide, 127, 1)).astype(BF)


def data_kernel(place, wown, wgot, own, got, other, keep, send, planes, peak):
    j = place[0]
    zero = jnp.zeros((3, 32, 128), BF)
    for slot in range(4):
        planes[slot, 0] = zero
        planes[slot, 9] = zero

    def fill(row):
        for s in range(3):
            put(planes, s + j, row + 1, jnp.concatenate([own[s, row], got[s, row]], axis=0))
        near = jnp.concatenate([other[0, j, row], other[1, j, row]], axis=0)
        put(planes, 3 * (1 - j), row + 1, near)

    for step in range(8):
        fill(step)
    peak[...] = jnp.zeros_like(peak)
    turned = iota((128, 128), 0) ^ (16 * place[1])
    pick = jnp.where(turned == iota((128, 128), 1), 1.0, 0.0).astype(BF)
    tiles = []
    for g in range(7):
        rows = []
        for s in range(4):
            t = 26 - 4 * g - s
            rows += [wown[t], wgot[t]] if t >= 0 else [jnp.zeros((32, 128), BF)]
        tile = lax.dot_general(
            pick, jnp.concatenate(rows, axis=0), NT, preferred_element_type=F32
        )
        tiles.append(tile.astype(BF))
    lhs = jnp.concatenate(tiles, axis=1)

    def window(plane, row):
        flat = planes[pl.ds(plane, 3), pl.ds(row, 3)].reshape(864, 128)
        return jnp.concatenate([flat, jnp.zeros((32, 128), BF)], axis=0)

    def row_pair(step):
        p, h = step // 4, 2 * (step % 4)
        rhs = jnp.concatenate([window(p, h), window(p, h + 1)], axis=1)
        res = jnp.dot(lhs, rhs, preferred_element_type=F32)
        at = (p * 8 + h) * 16
        for m in range(8):
            out = send if m % 2 else keep
            rows = pl.ds(m // 2 * 256 + at, 16)
            out[rows] = res[16 * m : 16 * m + 16, :128]
            rows = pl.ds(m // 2 * 256 + at + 16, 16)
            out[rows] = res[16 * m : 16 * m + 16, 128:]
        sizes = jnp.maximum(jnp.abs(res[:, :128]), jnp.abs(res[:, 128:]))
        peak[...] = jnp.maximum(peak[...], jnp.max(sizes.reshape(16, 8, 128), axis=0))

    for step in range(8):
        row_pair(step)
    size = size_of(peak[...])
    scale = jnp.exp2(14.0 - size)

    def bring(step):
        rows = pl.ds(step * 64, 64)
        send[rows] = (send[rows].reshape(8, 8, 128) * scale).reshape(64, 128)

    for step in range(16):
        bring(step)
    send[1024:1032] = size
    send[1032:1040] = size


def volume_kernel(
    place, wown, wgot, vown, vother, cown, cgot, cother, rkeep, rsend, taps, planes, cot, resp, acc
):
    j = place[0]
    cot[...] = jnp.zeros_like(cot)
    resp[...] = jnp.zeros_like(resp)
    half = pl.ds(pl.multiple_of(64 * j, 64), 64)

    def fill(row):
        for s in range(3):
            put(planes, 3 * j + s, row, vown[:, s, row].reshape(128, 128))
            put(planes, 3 * (1 - j) + s, row, vother[:, s, row].reshape(128, 128))
        for s in range(2):
            cot[2 + 2 * j + s, row + 1] = jnp.concatenate(
                [cown[s + 1 - j, row], cgot[s + 1 - j, row]], axis=0
            )
            cot[4 - 2 * j + s, row + 1] = jnp.concatenate(
                [cother[0, s, row], cother[1, s, row]], axis=0
            )

    for step in range(8):
        fill(step)

    weights = jnp.concatenate(
        [
            jnp.concatenate(
                [jnp.concatenate([wown[3 * ab + c], wgot[3 * ab + c]], axis=0) for c in range(3)],
                axis=1,
            )
            for ab in range(9)
        ],
        axis=0,
    )

    def row_pair(step):
        h = 2 * step
        for q in range(4):
            reach = [a for a in range(3) if 0 <= q - a < 2]
            lhs = weights[96 * reach[0] : 96 * reach[-1] + 96]
            first = planes[2 * j + q, h].reshape(384, 128)
            second = planes[2 * j + q, h + 1].reshape(384, 128)
            res = jnp.dot(
                lhs, jnp.concatenate([first, second], axis=1), preferred_element_type=F32
            )
            for n, a in enumerate(reach):
                for b in range(3):
                    at = 96 * n + 32 * b
                    resp[q - a, h + 2 - b] += res[at : at + 32, :128]
                    resp[q - a, h + 3 - b] += res[at : at + 32, 128:]

    for step in range(4):
        row_pair(step)
    peak = jnp.zeros((8, 128), F32)
    for p in range(2):
        for h in range(8):
            at = (p * 8 + h) * 16
            rkeep[at : at + 16] = resp[p, h + 1, :16]
            part = resp[p, h + 1, 16:]
            peak = jnp.maximum(peak, jnp.max(jnp.abs(part).reshape(2, 8, 128), axis=0))
    size = size_of(peak)
    scale = jnp.exp2(14.0 - size)
    for p in range(2):
        for h in range(8):
            at = (p * 8 + h) * 16
            part = resp[p, h + 1, 16:].reshape(2, 8, 128) * scale
            rsend[at : at + 16] = part.reshape(16, 128)
    rsend[256:264] = size
    rsend[264:272] = size

    acc[...] = jnp.zeros_like(acc)
    for q in range(6):
        low, high = max(0, 2 - q), min(2, 5 - q)
        lhs, rhs = [], []
        for h in range(8):
            grads = cot[q + low : q + high + 1, h : h + 3]
            lhs.append(grads.reshape(96 * (high - low + 1), 128))
            shifted = planes[q, h, :, half].reshape(192, 128)
            rhs.append(jnp.concatenate([shifted, jnp.zeros((64, 128), BF)], axis=0))
        res = lax.dot_general(
            jnp.concatenate(lhs, axis=1),
            jnp.concatenate(rhs, axis=1),
            NT,
            preferred_element_type=F32,
        )
        acc[96 * low : 96 * high + 96] += res
    for side in range(2):
        tiles, third = [], []
        for ab in range(9):
            rows = pl.ds(32 * ab + 16 * side, 16)
            tiles.append(acc[rows, :128])
            third.append(acc[rows, 128:])
        for n in range(4):
            tiles.append(third[2 * n] + pltpu.roll(third[2 * n + 1], 64, 1))
        tiles.append(third[8])
        for r, tile in enumerate(tiles):
            at = 32 * r + 16 * side
            taps[at : at + 16] = tile
    taps[448:512] = jnp.zeros((64, 128), F32)


def sum_kernel(factor, place, parts, out):
    total = parts[0]
    for n in range(1, 16):
        total = total + parts[n]
    out[...] = (total * factor).astype(BF)


def place_kernel(place, own, other, out):
    j = place[0]
    lane, n = iota((128, 512), 0), iota((128, 512), 1)
    y, z, i, s = n % 256 // 32, n % 32 // 16, n % 16, n // 256
    source = s * 64 + y % 4 * 16 + i
    total = jnp.zeros((224, 512), F32)
    for core, ref in enumerate((own, other)):
        for side in range(2):
            hit = (lane == source) & (y // 4 == (j ^ core)) & (z == side)
            pick = jnp.where(hit, 1.0, 0.0).astype(BF)
            part = ref[:14, side].reshape(224, 128)
            total = total + jnp.dot(part, pick, preferred_element_type=F32)
    for r in range(14):
        for s in range(2):
            ab, c = (r, s) if r < 9 else (2 * (r - 9) + s, 2)
            if ab > 8:
                continue
            t = (2 - ab // 3) * 9 + (2 - ab % 3) * 3 + c
            out[t] = total[16 * r : 16 * r + 16, 256 * s : 256 * s + 256].astype(BF)


def grow(value, power):
    return value.astype(F32) * jnp.exp2(power.astype(F32) - 14.0)


def split(total, power):
    count = total.shape[0] // 2
    send = (total[1::2] * jnp.exp2(14.0 - power)).reshape(count * 256, 128)
    return total[::2], jnp.concatenate([send, jnp.broadcast_to(power, (16, 128))])


def exchange(total, send, turn):
    got = lax.ppermute(send.astype(F16), "y", [(i, i ^ turn) for i in range(8)])
    return merge(total, send, got)


def merge(total, send, got):
    count = total.shape[0]
    theirs = got[256 * count : 256 * count + 1]
    total = total + grow(got[: 256 * count], theirs).reshape(count, 256, 128)
    return total, jnp.maximum(send[256 * count : 256 * count + 1], theirs.astype(F32)) + 1.0


def local(volume, filters, cotangent):
    depth, height, width = volume.shape[1:]
    cells = depth * height * width * lax.axis_size("xz") * lax.axis_size("co")
    chips = lax.axis_size("xz")
    core = lax.axis_index("co")
    place = jnp.stack([core, lax.axis_index("y"), lax.axis_index("zh")]).astype(jnp.int32)
    swap = [(0, 1), (1, 0)]

    fields = jnp.transpose(jnp.stack([volume, cotangent]), (0, 2, 3, 1, 4))
    near = [(2 * i + 1, 2 * i + 2) for i in range(chips - 1)]
    near = near + [(t, s) for s, t in near]

    rims = lax.ppermute(
        lax.dynamic_index_in_dim(fields, core, 1), ("xz", "co"), near
    )
    fields = jnp.where(
        core == 0,
        jnp.concatenate([rims, fields], axis=1),
        jnp.concatenate([fields, rims], axis=1),
    )
    slab, grad = fields[0], fields[1]

    tap_blocks = jnp.transpose(filters, (1, 2, 3, 0, 4)).reshape(27, 16, 256)
    wown, wsend = call(
        pack_kernel, [jax.ShapeDtypeStruct((27, 16, 128), BF)] * 2, [place, tap_blocks]
    )
    pair = lax.ppermute(
        jnp.concatenate([grad.reshape(384, 128), wsend.reshape(432, 128)]), "zh", swap
    )
    grad_got = pair[:384].reshape(3, 8, 16, 128)
    wgot = pair[384:].reshape(27, 16, 128)
    both = jnp.stack([grad, grad_got])
    grad_other = lax.ppermute(jnp.where(core == 0, both[:, 1:], both[:, :2]), "co", swap)
    vol = lax.all_to_all(jnp.broadcast_to(slab[None], (8, 3, 8, 16, 128)), "y", 0, 0)
    vol, grad_other = lax.optimization_barrier((vol, grad_other))
    vol_other = lax.ppermute(vol, "co", swap)
    data_keep, data_send = call(
        data_kernel,
        [jax.ShapeDtypeStruct((1024, 128), F32), jax.ShapeDtypeStruct((1040, 128), F32)],
        [place, wown, wgot, grad, grad_got, grad_other],
        [pltpu.VMEM((4, 10, 3, 32, 128), BF), pltpu.VMEM((8, 128), F32)],
        micros=10,
    )
    vol_other, data_keep, data_send = lax.optimization_barrier((vol_other, data_keep, data_send))
    data_got = lax.ppermute(data_send.astype(F16), "y", [(i, i ^ 1) for i in range(8)])
    rkeep, rsend, taps = call(
        volume_kernel,
        [jax.ShapeDtypeStruct((rows, 128), F32) for rows in (256, 272, 512)],
        [place, wown, wgot, vol, vol_other, grad, grad_got, grad_other],
        [
            pltpu.VMEM((6, 8, 3, 128, 128), BF),
            pltpu.VMEM((8, 10, 32, 128), BF),
            pltpu.VMEM((2, 10, 32, 128), F32),
            pltpu.VMEM((288, 256), F32),
        ],
        micros=8,
    )
    kernel = lax.all_to_all(taps.reshape(16, 32, 128), "xz", 0, 0)
    got = lax.ppermute(rsend.astype(F16), "zh", swap)

    kernel, data_got1 = lax.optimization_barrier((kernel, data_got))
    kernel = call(
        functools.partial(sum_kernel, 1.0 / math.sqrt(cells)),
        jax.ShapeDtypeStruct((32, 128), BF),
        [place, kernel],
    )
    data, power = merge(data_keep.reshape(4, 256, 128), data_send, data_got1)
    data, power = exchange(*split(data, power), 2)
    data_keep, data_send = split(data, power)
    data_got = lax.ppermute(data_send.astype(F16), "y", [(i, i ^ 4) for i in range(8)])

    halves = kernel.reshape(2, 16, 128)
    halves = jnp.where(lax.axis_index("zh") == 0, halves, halves[::-1])
    kernel = jnp.broadcast_to(halves[None], (16, 2, 16, 128)).reshape(32, 16, 128)
    kernel = lax.all_to_all(kernel, ("xz", "zh"), 0, 0).reshape(16, 2, 16, 128)
    kernel, got = lax.optimization_barrier((kernel, got))
    response = (rkeep + grow(got[:256], got[256:257])).reshape(2, 8, 16, 128)
    kernel_other = lax.ppermute(kernel, "co", swap)
    kernel_other, data_got = lax.optimization_barrier((kernel_other, data_got))
    data, power = merge(data_keep, data_send, data_got)
    data = data.reshape(2, 8, 16, 128)
    placed = call(
        place_kernel, jax.ShapeDtypeStruct((27, 16, 256), BF), [place, kernel, kernel_other]
    )
    order = (2, 0, 1, 3)
    return (
        jnp.transpose(response.astype(BF), order),
        jnp.transpose(data.astype(BF), order),
        jnp.transpose(placed.reshape(3, 3, 3, 16, 256), (3, 0, 1, 2, 4)),
    )


def solution(mesh):
    grid = Mesh(mesh.devices.reshape(16, 2, 8, 2), ("xz", "co", "y", "zh"))
    cells = P(("y", "zh"), ("xz", "co"), None, None)
    kernel = P(("y", "zh"), None, None, None, None)
    return jax.shard_map(
        local,
        mesh=grid,
        in_specs=(cells, kernel, cells),
        out_specs=(cells, cells, kernel),
        check_vma=False,
    )
```

```python
import functools
import math

import jax
import jax.numpy as jnp
from jax import lax
from jax.experimental import pallas as pl
from jax.experimental.pallas import tpu as pltpu
from jax.sharding import Mesh
from jax.sharding import PartitionSpec as P

BF = jnp.bfloat16
F32 = jnp.float32
F16 = jnp.float16
VMEM = pl.BlockSpec(memory_space=pltpu.VMEM)
SMEM = pl.BlockSpec(memory_space=pltpu.SMEM)
PARAMS = pltpu.CompilerParams(vmem_limit_bytes=48 * 1024 * 1024)
NT = (((1,), (1,)), ((), ()))


def call(kernel, out_shape, operands, scratch=(), micros=1):
    return pl.pallas_call(
        kernel,
        out_shape=out_shape,
        in_specs=[SMEM] + [VMEM] * (len(operands) - 1),
        out_specs=jax.tree.map(lambda _: VMEM, out_shape),
        scratch_shapes=list(scratch),
        compiler_params=PARAMS,
        cost_estimate=pl.CostEstimate(
            flops=int(micros * 1e9), bytes_accessed=1 << 18, transcendentals=0
        ),
    )(*operands)


def iota(shape, dim):
    return lax.broadcasted_iota(jnp.int32, shape, dim)


def size_of(peak):
    most = jnp.max(jnp.max(peak, axis=0, keepdims=True), axis=1, keepdims=True)
    power = jnp.floor(jnp.log2(jnp.clip(most, 2.0**-100, 2.0**100)))
    return jnp.broadcast_to(power, (8, 128))


def pack_kernel(place, fil, own, send):
    zh = place[2]
    lane = iota((256, 256), 1)
    wanted = (lane % 128) // 16 * 32 + (zh ^ (lane // 128)) * 16 + lane % 16
    pick = jnp.where(iota((256, 256), 0) == wanted, 1.0, 0.0).astype(BF)
    res = jnp.dot(fil[...].reshape(432, 256), pick, preferred_element_type=F32).astype(BF)
    own[...] = res[:, :128].reshape(27, 16, 128)
    send[...] = res[:, 128:].reshape(27, 16, 128)


def put(dst, slot, row, block):
    wide = block.astype(F32)
    lane = iota(block.shape, 1)
    dst[slot, row, 0] = jnp.where(lane == 0, 0.0, pltpu.roll(wide, 1, 1)).astype(BF)
    dst[slot, row, 1] = block
    dst[slot, row, 2] = jnp.where(lane == 127, 0.0, pltpu.roll(wide, 127, 1)).astype(BF)


def data_kernel(place, wown, wgot, own, got, other, keep, send, planes, peak):
    j = place[0]
    zero = jnp.zeros((3, 32, 128), BF)
    for slot in range(4):
        planes[slot, 0] = zero
        planes[slot, 9] = zero

    def fill(row):
        for s in range(3):
            put(planes, s + j, row + 1, jnp.concatenate([own[s, row], got[s, row]], axis=0))
        near = jnp.concatenate([other[0, j, row], other[1, j, row]], axis=0)
        put(planes, 3 * (1 - j), row + 1, near)

    for step in range(8):
        fill(step)
    peak[...] = jnp.zeros_like(peak)
    turned = iota((128, 128), 0) ^ (16 * place[1])
    pick = jnp.where(turned == iota((128, 128), 1), 1.0, 0.0).astype(BF)
    tiles = []
    for g in range(7):
        rows = []
        for s in range(4):
            t = 26 - 4 * g - s
            rows += [wown[t], wgot[t]] if t >= 0 else [jnp.zeros((32, 128), BF)]
        tile = lax.dot_general(
            pick, jnp.concatenate(rows, axis=0), NT, preferred_element_type=F32
        )
        tiles.append(tile.astype(BF))
    lhs = jnp.concatenate(tiles, axis=1)

    def window(plane, row):
        flat = planes[pl.ds(plane, 3), pl.ds(row, 3)].reshape(864, 128)
        return jnp.concatenate([flat, jnp.zeros((32, 128), BF)], axis=0)

    def row_pair(step):
        p, h = step // 4, 2 * (step % 4)
        rhs = jnp.concatenate([window(p, h), window(p, h + 1)], axis=1)
        res = jnp.dot(lhs, rhs, preferred_element_type=F32)
        for m in range(8):
            out = send if m % 2 else keep
            rows = pl.ds(m // 2 * 256 + p * 8 + h, 16, stride=16)
            out[rows] = res[16 * m : 16 * m + 16, :128]
            rows = pl.ds(m // 2 * 256 + p * 8 + h + 1, 16, stride=16)
            out[rows] = res[16 * m : 16 * m + 16, 128:]
        sizes = jnp.maximum(jnp.abs(res[:, :128]), jnp.abs(res[:, 128:]))
        peak[...] = jnp.maximum(peak[...], jnp.max(sizes.reshape(16, 8, 128), axis=0))

    for step in range(8):
        row_pair(step)
    size = size_of(peak[...])
    scale = jnp.exp2(14.0 - size)

    def bring(step):
        rows = pl.ds(step * 64, 64)
        send[rows] = (send[rows].reshape(8, 8, 128) * scale).reshape(64, 128)

    for step in range(16):
        bring(step)
    send[1024:1032] = size
    send[1032:1040] = size


def volume_kernel(
    place, wown, wgot, vown, vother, cown, cgot, cother, rkeep, rsend, taps, planes, cot, resp, acc
):
    j = place[0]
    cot[...] = jnp.zeros_like(cot)
    resp[...] = jnp.zeros_like(resp)
    half = pl.ds(pl.multiple_of(64 * j, 64), 64)

    def fill(row):
        for s in range(3):
            put(planes, 3 * j + s, row, vown[:, s, row].reshape(128, 128))
            put(planes, 3 * (1 - j) + s, row, vother[:, s, row].reshape(128, 128))
        for s in range(2):
            cot[2 + 2 * j + s, row + 1] = jnp.concatenate(
                [cown[s + 1 - j, row], cgot[s + 1 - j, row]], axis=0
            )
            cot[4 - 2 * j + s, row + 1] = jnp.concatenate(
                [cother[0, s, row], cother[1, s, row]], axis=0
            )

    for step in range(8):
        fill(step)

    weights = jnp.concatenate(
        [
            jnp.concatenate(
                [jnp.concatenate([wown[3 * ab + c], wgot[3 * ab + c]], axis=0) for c in range(3)],
                axis=1,
            )
            for ab in range(9)
        ],
        axis=0,
    )

    def row_pair(step):
        h = 2 * step
        for q in range(4):
            reach = [a for a in range(3) if 0 <= q - a < 2]
            lhs = weights[96 * reach[0] : 96 * reach[-1] + 96]
            first = planes[2 * j + q, h].reshape(384, 128)
            second = planes[2 * j + q, h + 1].reshape(384, 128)
            res = jnp.dot(
                lhs, jnp.concatenate([first, second], axis=1), preferred_element_type=F32
            )
            for n, a in enumerate(reach):
                for b in range(3):
                    at = 96 * n + 32 * b
                    resp[q - a, h + 2 - b] += res[at : at + 32, :128]
                    resp[q - a, h + 3 - b] += res[at : at + 32, 128:]

    for step in range(4):
        row_pair(step)
    peak = jnp.zeros((8, 128), F32)
    for p in range(2):
        for h in range(8):
            at = (p * 8 + h) * 16
            rkeep[at : at + 16] = resp[p, h + 1, :16]
            part = resp[p, h + 1, 16:]
            peak = jnp.maximum(peak, jnp.max(jnp.abs(part).reshape(2, 8, 128), axis=0))
    size = size_of(peak)
    scale = jnp.exp2(14.0 - size)
    for p in range(2):
        for h in range(8):
            at = (p * 8 + h) * 16
            part = resp[p, h + 1, 16:].reshape(2, 8, 128) * scale
            rsend[at : at + 16] = part.reshape(16, 128)
    rsend[256:264] = size
    rsend[264:272] = size

    acc[...] = jnp.zeros_like(acc)
    for q in range(6):
        low, high = max(0, 2 - q), min(2, 5 - q)
        lhs, rhs = [], []
        for h in range(8):
            grads = cot[q + low : q + high + 1, h : h + 3]
            lhs.append(grads.reshape(96 * (high - low + 1), 128))
            shifted = planes[q, h, :, half].reshape(192, 128)
            rhs.append(jnp.concatenate([shifted, jnp.zeros((64, 128), BF)], axis=0))
        res = lax.dot_general(
            jnp.concatenate(lhs, axis=1),
            jnp.concatenate(rhs, axis=1),
            NT,
            preferred_element_type=F32,
        )
        acc[96 * low : 96 * high + 96] += res
    for side in range(2):
        tiles, third = [], []
        for ab in range(9):
            rows = pl.ds(32 * ab + 16 * side, 16)
            tiles.append(acc[rows, :128])
            third.append(acc[rows, 128:])
        for n in range(4):
            tiles.append(third[2 * n] + pltpu.roll(third[2 * n + 1], 64, 1))
        tiles.append(third[8])
        for r, tile in enumerate(tiles):
            at = 32 * r + 16 * side
            taps[at : at + 16] = tile
    taps[448:512] = jnp.zeros((64, 128), F32)


def sum_kernel(factor, place, parts, out):
    total = parts[0]
    for n in range(1, 16):
        total = total + parts[n]
    out[...] = (total * factor).astype(BF)


def place_kernel(place, own, other, out):
    j = place[0]
    lane, n = iota((128, 512), 0), iota((128, 512), 1)
    y, z, i, s = n % 256 // 32, n % 32 // 16, n % 16, n // 256
    source = s * 64 + y % 4 * 16 + i
    total = jnp.zeros((224, 512), F32)
    for core, ref in enumerate((own, other)):
        for side in range(2):
            hit = (lane == source) & (y // 4 == (j ^ core)) & (z == side)
            pick = jnp.where(hit, 1.0, 0.0).astype(BF)
            part = ref[:14, side].reshape(224, 128)
            total = total + jnp.dot(part, pick, preferred_element_type=F32)
    for r in range(14):
        for s in range(2):
            ab, c = (r, s) if r < 9 else (2 * (r - 9) + s, 2)
            if ab > 8:
                continue
            t = (2 - ab // 3) * 9 + (2 - ab % 3) * 3 + c
            out[t] = total[16 * r : 16 * r + 16, 256 * s : 256 * s + 256].astype(BF)


def grow(value, power):
    return value.astype(F32) * jnp.exp2(power.astype(F32) - 14.0)


def split(total, power):
    count = total.shape[0] // 2
    send = (total[1::2] * jnp.exp2(14.0 - power)).reshape(count * 256, 128)
    return total[::2], jnp.concatenate([send, jnp.broadcast_to(power, (16, 128))])


def exchange(total, send, turn):
    got = lax.ppermute(send.astype(F16), "y", [(i, i ^ turn) for i in range(8)])
    return merge(total, send, got)


def merge(total, send, got):
    count = total.shape[0]
    theirs = got[256 * count : 256 * count + 1]
    total = total + grow(got[: 256 * count], theirs).reshape(count, 256, 128)
    return total, jnp.maximum(send[256 * count : 256 * count + 1], theirs.astype(F32)) + 1.0


def local(volume, filters, cotangent):
    depth, height, width = volume.shape[1:]
    cells = depth * height * width * lax.axis_size("xz") * lax.axis_size("co")
    chips = lax.axis_size("xz")
    core = lax.axis_index("co")
    place = jnp.stack([core, lax.axis_index("y"), lax.axis_index("zh")]).astype(jnp.int32)
    swap = [(0, 1), (1, 0)]

    fields = jnp.transpose(jnp.stack([volume, cotangent]), (0, 2, 3, 1, 4))
    near = [(2 * i + 1, 2 * i + 2) for i in range(chips - 1)]
    near = near + [(t, s) for s, t in near]

    rims = lax.ppermute(
        lax.dynamic_index_in_dim(fields, core, 1), ("xz", "co"), near
    )
    fields = jnp.where(
        core == 0,
        jnp.concatenate([rims, fields], axis=1),
        jnp.concatenate([fields, rims], axis=1),
    )
    slab, grad = fields[0], fields[1]

    tap_blocks = jnp.transpose(filters, (1, 2, 3, 0, 4)).reshape(27, 16, 256)
    wown, wsend = call(
        pack_kernel, [jax.ShapeDtypeStruct((27, 16, 128), BF)] * 2, [place, tap_blocks]
    )
    pair = lax.ppermute(
        jnp.concatenate([grad.reshape(384, 128), wsend.reshape(432, 128)]), "zh", swap
    )
    grad_got = pair[:384].reshape(3, 8, 16, 128)
    wgot = pair[384:].reshape(27, 16, 128)
    both = jnp.stack([grad, grad_got])
    grad_other = lax.ppermute(jnp.where(core == 0, both[:, 1:], both[:, :2]), "co", swap)
    vol = lax.all_to_all(jnp.broadcast_to(slab[None], (8, 3, 8, 16, 128)), "y", 0, 0)
    vol, grad_other = lax.optimization_barrier((vol, grad_other))
    vol_other = lax.ppermute(vol, "co", swap)
    data_keep, data_send = call(
        data_kernel,
        [jax.ShapeDtypeStruct((1024, 128), F32), jax.ShapeDtypeStruct((1040, 128), F32)],
        [place, wown, wgot, grad, grad_got, grad_other],
        [pltpu.VMEM((4, 10, 3, 32, 128), BF), pltpu.VMEM((8, 128), F32)],
        micros=10,
    )
    vol_other, data_keep, data_send = lax.optimization_barrier((vol_other, data_keep, data_send))
    data_got = lax.ppermute(data_send.astype(F16), "y", [(i, i ^ 1) for i in range(8)])
    rkeep, rsend, taps = call(
        volume_kernel,
        [jax.ShapeDtypeStruct((rows, 128), F32) for rows in (256, 272, 512)],
        [place, wown, wgot, vol, vol_other, grad, grad_got, grad_other],
        [
            pltpu.VMEM((6, 8, 3, 128, 128), BF),
            pltpu.VMEM((8, 10, 32, 128), BF),
            pltpu.VMEM((2, 10, 32, 128), F32),
            pltpu.VMEM((288, 256), F32),
        ],
        micros=8,
    )
    kernel = lax.all_to_all(taps.reshape(16, 32, 128), "xz", 0, 0)
    got = lax.ppermute(rsend.astype(F16), "zh", swap)

    kernel, data_got1 = lax.optimization_barrier((kernel, data_got))
    kernel = call(
        functools.partial(sum_kernel, 1.0 / math.sqrt(cells)),
        jax.ShapeDtypeStruct((32, 128), BF),
        [place, kernel],
    )
    data, power = merge(data_keep.reshape(4, 256, 128), data_send, data_got1)
    data, power = exchange(*split(data, power), 2)
    data_keep, data_send = split(data, power)
    data_got = lax.ppermute(data_send.astype(F16), "y", [(i, i ^ 4) for i in range(8)])

    halves = kernel.reshape(2, 16, 128)
    halves = jnp.where(lax.axis_index("zh") == 0, halves, halves[::-1])
    kernel = jnp.broadcast_to(halves[None], (16, 2, 16, 128)).reshape(32, 16, 128)
    kernel = lax.all_to_all(kernel, ("xz", "zh"), 0, 0).reshape(16, 2, 16, 128)
    kernel, got = lax.optimization_barrier((kernel, got))
    response = (rkeep + grow(got[:256], got[256:257])).reshape(2, 8, 16, 128)
    kernel_other = lax.ppermute(kernel, "co", swap)
    kernel_other, data_got = lax.optimization_barrier((kernel_other, data_got))
    data, power = merge(data_keep, data_send, data_got)
    data = data.reshape(16, 2, 8, 128)
    placed = call(
        place_kernel, jax.ShapeDtypeStruct((27, 16, 256), BF), [place, kernel, kernel_other]
    )
    order = (2, 0, 1, 3)
    return (
        jnp.transpose(response.astype(BF), order),
        data.astype(BF),
        jnp.transpose(placed.reshape(3, 3, 3, 16, 256), (3, 0, 1, 2, 4)),
    )


def solution(mesh):
    grid = Mesh(mesh.devices.reshape(16, 2, 8, 2), ("xz", "co", "y", "zh"))
    cells = P(("y", "zh"), ("xz", "co"), None, None)
    kernel = P(("y", "zh"), None, None, None, None)
    return jax.shard_map(
        local,
        mesh=grid,
        in_specs=(cells, kernel, cells),
        out_specs=(cells, cells, kernel),
        check_vma=False,
    )
```
